32 devices in a mesh: seg: 4 (over y, core), sec: 8 (over z, x).
Axes of the slice: x: 2, y: 2, z: 4, core: 2. Of those that a mesh axis runs over, the one named last changes fastest.
Arguments:
- psi_init: float32 [4, 8, 256, 256], P('seg', 'sec'), may hold values from -6 to 6
- boundary_env: float32 [8, 18, 256, 256], P('sec')
- right_env: float32 [4, 8, 18, 256, 256], P('seg', 'sec')
- transfer_blocks: float32 [4, 8, 256, 256], P('seg', 'sec')
- transfer_mix: float32 [4, 18, 18], P('seg')
- hop_left: float32 [4, 8, 256, 256], P('seg', 'sec'), may hold values from -0.75 to 0.75
- hop_right: float32 [4, 8, 256, 256], P('seg', 'sec'), may hold values from -0.75 to 0.75
- block_sizes: int32 [4, 2, 8], P('seg'), may hold values from 64 to 256, as said below
- sources: int32 [4, 8], P('seg'), may hold values from 0 to 7, each once within a row
Outputs:
- state: float32 [4, 8, 256, 256], P('seg', 'sec')
The draws below stay inside these ranges and needn't reach their ends.
Inputs may be any that keep to these rules, and one draw needn't show every extreme that they name: `sources`: each block number appears once in a segment's list. `block_sizes`: each segment has a block with 256 live rows and one with 256 live columns.
All inputs are finite; a program needn't handle non-finite values.
Results may differ from the reference program's by a relative error of at most 0.0003.
Values sent between devices are 32-bit elements; how exact they have to be, the bound alone decides.
A program may use at most 128 MiB of HBM per device.

```python
import jax
import jax.numpy as jnp
from jax import lax

P_SIZE = 256
W = 18
DAV = 2
BLK = 8
SEGS = 4


def env_law(key, shape):
    key_diag, key_rest = jax.random.split(key)
    rows = lax.broadcasted_iota(jnp.int32, shape, len(shape) - 2)
    cols = lax.broadcasted_iota(jnp.int32, shape, len(shape) - 1)
    unit = (rows == cols).astype(jnp.float32)
    diag_vals = jax.random.uniform(key_diag, shape[:-1], jnp.float32, 0.5, 2.0)
    noise = jax.random.normal(key_rest, shape, jnp.float32) * (0.5 / P_SIZE ** 0.5)
    return diag_vals[..., :, None] * unit + noise


def near_unit(key, shape, spread):
    rows = lax.broadcasted_iota(jnp.int32, shape, len(shape) - 2)
    cols = lax.broadcasted_iota(jnp.int32, shape, len(shape) - 1)
    unit = (rows == cols).astype(jnp.float32)
    return unit + jax.random.normal(key, shape, jnp.float32) * (spread / shape[-1] ** 0.5)


def draw_boundary_env(key, part):
    return env_law(jax.random.fold_in(key, 11), (BLK, W, P_SIZE, P_SIZE))


def draw_right_env(key, part):
    return env_law(jax.random.fold_in(key, 12), (SEGS, BLK, W, P_SIZE, P_SIZE))


def draw_transfer_blocks(key, part):
    return near_unit(jax.random.fold_in(key, 13), (SEGS, BLK, P_SIZE, P_SIZE), 0.3)


def draw_transfer_mix(key, part):
    return near_unit(jax.random.fold_in(key, 14), (SEGS, W, W), 0.3)


def draw_block_sizes(key, part):
    key_vals, key_pick = jax.random.split(jax.random.fold_in(key, 15))
    values = jax.random.randint(key_vals, (SEGS, 2, BLK), P_SIZE // 4, P_SIZE + 1)
    chosen = jax.random.randint(key_pick, (SEGS, 2, 1), 0, BLK)
    filled = lax.broadcasted_iota(jnp.int32, (SEGS, 2, BLK), 2) == chosen
    return jnp.where(filled, P_SIZE, values).astype(jnp.int32)


def block_levels(rng, extent, shards, smallest, top_value):
    loudness, own = 1.0, jax.random.fold_in(rng, 6)
    for position, blocks in shards:
        heights = jnp.exp(jax.random.uniform(jax.random.fold_in(own, position), (blocks,), jnp.float32, smallest / len(shards), top_value / len(shards)))
        loudness = loudness * jnp.repeat(heights, extent[position] // blocks).reshape([-1 if axis == position else 1 for axis in range(len(extent))])
    return loudness


def normal_values(stream_key, extent, scale, reach, shards=(), held_as=jnp.bfloat16):
    array = scale * jax.random.normal(stream_key, extent, jnp.float32)
    if shards:
        array = array * block_levels(stream_key, extent, shards, -0.22, 0.18)
    return jnp.clip(array, -reach, reach).astype(held_as)


def setup_inputs(seed: int = 0) -> dict:
    splits = jax.random.split(jax.random.key(seed), 10)
    psi_init = normal_values(splits[0], (SEGS, BLK, P_SIZE, P_SIZE), 1.0, 6.0, ((0, 4), (1, 8)), jnp.float32)
    boundary_env = draw_boundary_env(jax.random.fold_in(splits[9], 71), 0)
    right_env = draw_right_env(jax.random.fold_in(splits[9], 71), 0)
    transfer_blocks = draw_transfer_blocks(jax.random.fold_in(splits[9], 71), 0)
    transfer_mix = draw_transfer_mix(jax.random.fold_in(splits[9], 71), 0)
    hop_left = normal_values(splits[5], (SEGS, BLK, P_SIZE, P_SIZE), (P_SIZE // 4) ** -0.5, 0.75, ((0, 4), (1, 8)), jnp.float32)
    hop_right = normal_values(splits[6], (SEGS, BLK, P_SIZE, P_SIZE), (P_SIZE // 4) ** -0.5, 0.75, ((0, 4), (1, 8)), jnp.float32)
    block_sizes = draw_block_sizes(jax.random.fold_in(splits[9], 71), 0)
    sources = jax.vmap(lambda own: jax.random.permutation(own, BLK))(jax.random.split(splits[8], SEGS)).reshape((SEGS, BLK)).astype(jnp.int32)
    return dict(psi_init=psi_init, boundary_env=boundary_env, right_env=right_env, transfer_blocks=transfer_blocks, transfer_mix=transfer_mix, hop_left=hop_left, hop_right=hop_right, block_sizes=block_sizes, sources=sources)


HIGH = lax.Precision.HIGHEST
EPSILON = 1e-06

def product(left, right):
    return jnp.matmul(left, right, precision=HIGH)

def build_env(prefix_mix, prefix_blocks, boundary):
    turned = product(product(jnp.swapaxes(prefix_blocks, 1, 2)[:, None], boundary), prefix_blocks[:, None])
    return jnp.einsum('vw,bvij->bwij', prefix_mix, turned, precision=HIGH)

def solve_window(initial, left_env, right_side, left_hop, right_hop, live_sizes, source_list):
    block_width = initial.shape[-1]
    places = lax.broadcasted_iota(jnp.int32, (1, block_width), 1)
    row_live = (places < live_sizes[0][:, None]).astype(jnp.float32)
    col_live = (places < live_sizes[1][:, None]).astype(jnp.float32)
    masking = row_live[:, :, None] * col_live[:, None, :]
    diagonal = jnp.einsum('bwi,bwj->bij', jnp.diagonal(left_env, axis1=2, axis2=3), jnp.diagonal(right_side, axis1=2, axis2=3), precision=HIGH)

    def apply_h(vector):
        local_part = lax.optimization_barrier(jnp.sum(product(product(left_env, vector[:, None]), right_side), axis=1))
        regrouped = product(vector, right_hop)[source_list]
        return masking * (local_part + product(left_hop, regrouped))
    vector = masking * initial
    vector = vector / jnp.sqrt(jnp.sum(vector * vector) + EPSILON)
    for turn_index in range(DAV):
        image_vec = apply_h(vector)
        rayleigh = jnp.sum(vector * image_vec)
        residue = image_vec - rayleigh * vector
        shifted = diagonal - rayleigh
        update = vector - residue * shifted / (shifted * shifted + 1.0)
        vector = update / jnp.sqrt(jnp.sum(update * update) + EPSILON)
    return vector * jnp.sqrt(jnp.float32(BLK * P_SIZE * P_SIZE))

def reference(psi_init, boundary_env, right_env, transfer_blocks, transfer_mix, hop_left, hop_right, block_sizes, sources):
    prefix_mix = jnp.eye(W, dtype=jnp.float32)
    prefix_blocks = jnp.broadcast_to(jnp.eye(P_SIZE, dtype=jnp.float32), (BLK, P_SIZE, P_SIZE))
    results = []
    for segment in range(SEGS):
        left_env = build_env(prefix_mix, prefix_blocks, boundary_env)
        results.append(solve_window(psi_init[segment], left_env, right_env[segment], hop_left[segment], hop_right[segment], block_sizes[segment], sources[segment]))
        prefix_mix = product(prefix_mix, transfer_mix[segment])
        prefix_blocks = product(prefix_blocks, transfer_blocks[segment])
    return jnp.stack(results)
```

```python
import functools
import math

import jax
import jax.numpy as jnp
from jax import lax
from jax.experimental import pallas as pl
from jax.experimental.pallas import tpu as pltpu
from jax.sharding import PartitionSpec as P

DAV = 2
EPSILON = 1e-06
HIGH = lax.Precision.HIGHEST
F32 = jnp.float32
BF16 = jnp.bfloat16
MESH = pl.DeviceIdType.MESH


def split(x):
    high = x.astype(BF16)
    return high, (x - high.astype(F32)).astype(BF16)


def left_cat(pair):
    high, low = pair
    return jnp.concatenate([high, high, low], axis=1)


def right_cat(pair):
    high, low = pair
    return jnp.concatenate([high, low, high], axis=0)


def dot(a, b):
    return jnp.dot(a, b, preferred_element_type=F32)


def exact(a, b, dims=((1,), (0,))):
    return lax.dot_general(a, b, (dims, ((), ())), precision=HIGH, preferred_element_type=F32)


def total(x):
    return jnp.sum(jnp.sum(x, axis=0, keepdims=True), axis=1, keepdims=True)


def octets(x):
    return jnp.sum(x.reshape(x.shape[0] // 8, 8, x.shape[1]), axis=0)


def kernel(
    nseg, nsec, W, N,
    sizes, sources, psi, boundary, right, own, mix, hop_left, hop_right,
    out,
    b_buf, r_buf, c_hi, c_lo, m_hi, m_lo, mixes, prefix, carry, diag_l, diag_r, diagonal, acc, vec,
    send_a, send_b, relay_a, relay_b, fwd_a, fwd_b, got_a, got_b,
    red0, red1, red2, red3, red4,
    load_sem, mix_send, mix_recv, chain_send, chain_recv,
    one_send, one_recv, two_send, two_recv, red_send, red_recv,
):
    seg, sec = lax.axis_index("seg"), lax.axis_index("sec")
    rows = N // nsec
    W8 = W * 8
    WP = mixes.shape[1]
    wide = -(-W // 8) * 8
    reds = (red0, red1, red2, red3, red4)
    sends, relays, fwds, gots = (send_a, send_b), (relay_a, relay_b), (fwd_a, fwd_b), (got_a, got_b)

    load_r = pltpu.make_async_copy(right, r_buf, load_sem.at[0])
    load_b = pltpu.make_async_copy(boundary, b_buf, load_sem.at[1])
    load_r.start()
    load_b.start()

    def other(index, step, count):
        return lax.rem(index + step, count)

    barrier = pltpu.get_barrier_semaphore()
    mixes[...] = jnp.zeros_like(mixes)
    mixes.at[seg][0:W, 0:W] = mix[...]
    for k in range(1, nsec):
        pl.semaphore_signal(barrier, inc=1, device_id={"sec": other(sec, k, nsec)}, device_id_type=MESH)
    for k in range(1, nseg):
        pl.semaphore_signal(barrier, inc=1, device_id={"seg": other(seg, k, nseg)}, device_id_type=MESH)

    @pl.when(seg == 0)
    def _():
        carry[...] = own[...]
        prefix[...] = jnp.where(
            lax.broadcasted_iota(jnp.int32, (N, N), 0) == lax.broadcasted_iota(jnp.int32, (N, N), 1), 1.0, 0.0
        )

    pl.semaphore_wait(barrier, nsec + nseg - 2)

    def mix_copy(k, slot):
        return pltpu.make_async_remote_copy(
            mixes.at[slot, pl.ds(0, wide)], mixes.at[slot, pl.ds(0, wide)],
            mix_send.at[k], mix_recv.at[k], device_id={"seg": other(seg, k, nseg)}, device_id_type=MESH,
        )

    for k in range(1, nseg):
        mix_copy(k, seg).start()

    halves = 2
    part = N // halves

    def chain_copy(i):
        return pltpu.make_async_remote_copy(
            carry.at[pl.ds(i * part, part)], prefix.at[pl.ds(i * part, part)],
            chain_send.at[i], chain_recv.at[i],
            device_id={"seg": lax.rem(seg + 1, nseg)}, device_id_type=MESH,
        )

    @pl.when(seg == 0)
    def _():
        for i in range(halves):
            chain_copy(i).start()

    def chain_step():
        for i in range(halves):
            chain_copy(i).wait_recv()

            @pl.when(seg < nseg - 1)
            def _():
                here = pl.ds(i * part, part)
                carry[here] = exact(prefix[here], own[...])
                chain_copy(i).start()

    def reduce_copy(r, k, slot):
        return pltpu.make_async_remote_copy(
            reds[r].at[slot], reds[r].at[slot], red_send.at[r, k], red_recv.at[r, k],
            device_id={"sec": other(sec, k, nsec)}, device_id_type=MESH,
        )

    def reduce_start(r, value):
        reds[r].at[sec][...] = jnp.broadcast_to(value, (8, 128))
        for k in range(1, nsec):
            reduce_copy(r, k, sec).start()

    def reduce_end(r):
        for k in range(1, nsec):
            reduce_copy(r, k, lax.rem(sec + nsec - k, nsec)).wait_recv()
        return jnp.sum(reds[r][...], axis=0)[0:1, 0:1]

    def one_copy(t, k, piece, slot):
        return pltpu.make_async_remote_copy(
            sends[t].at[piece], relays[t].at[slot], one_send.at[t, k], one_recv.at[t, k],
            device_id={"sec": other(sec, k, nsec)}, device_id_type=MESH,
        )

    def two_copy(t, k, piece, slot):
        return pltpu.make_async_remote_copy(
            fwds[t].at[piece], gots[t].at[slot], two_send.at[t, k], two_recv.at[t, k],
            device_id={"sec": other(sec, k, nsec)}, device_id_type=MESH,
        )

    def permute_start(t, value):
        sends[t][...] = value.reshape(nsec, rows, N)
        for k in range(1, nsec):
            one_copy(t, k, other(sec, k, nsec), sec).start()
        relays[t].at[sec][...] = sends[t].at[sec][...]

    def permute_turn(t):
        for k in range(1, nsec):
            one_copy(t, k, sec, lax.rem(sec + nsec - k, nsec)).wait_recv()
        for d in range(nsec):
            fwds[t][d] = relays[t][sources[0, d]]
        for k in range(1, nsec):
            two_copy(t, k, other(sec, k, nsec), sec).start()
        gots[t].at[sec][...] = fwds[t].at[sec][...]

    def permute_end(t):
        for k in range(1, nsec):
            two_copy(t, k, sec, lax.rem(sec + nsec - k, nsec)).wait_recv()
        return gots[t][...].reshape(N, N)

    places_i = lax.broadcasted_iota(jnp.int32, (N, N), 0)
    places_j = lax.broadcasted_iota(jnp.int32, (N, N), 1)

    def masked(x):
        return jnp.where((places_i < sizes[0, sec]) & (places_j < sizes[1, sec]), x, 0.0)

    hop_right_cat = right_cat(split(hop_right[...]))
    start = masked(psi[...])
    permute_start(0, dot(left_cat(split(start)), hop_right_cat))
    reduce_start(0, total(start * start))

    @pl.when((seg > 0) & (seg < 2))
    def _():
        chain_step()

    for k in range(1, nseg):
        mix_copy(k, lax.rem(seg + nseg - k, nseg)).wait_recv()
    prefix_mix = jnp.where(
        lax.broadcasted_iota(jnp.int32, (WP, WP), 0) == lax.broadcasted_iota(jnp.int32, (WP, WP), 1), 1.0, 0.0
    )
    for t in range(nseg - 1):
        prefix_mix = jnp.where(t < seg, exact(prefix_mix, mixes[t]), prefix_mix)
    spread = jnp.where(
        lax.broadcasted_iota(jnp.int32, (W8, WP), 0) // 8 == lax.broadcasted_iota(jnp.int32, (W8, WP), 1), 1.0, 0.0
    )
    mix_full = exact(exact(spread, prefix_mix), spread, ((1,), (1,)))
    same = (
        lax.broadcasted_iota(jnp.int32, (W8, W8), 0) % 8 == lax.broadcasted_iota(jnp.int32, (W8, W8), 1) % 8
    )
    k_hi, k_lo = split(jnp.where(same, mix_full, 0.0))
    load_r.wait()

    @pl.loop(0, N // 16)
    def _(c):
        here = pl.ds(pl.multiple_of(c * 16, 16), 16)
        chunk = r_buf[:, here, :]
        side = jnp.concatenate([chunk[:, 0:8].reshape(W8, N), chunk[:, 8:16].reshape(W8, N)], axis=1)
        s_hi, s_lo = split(side)
        mixed = dot(k_hi, s_hi) + (dot(k_hi, s_lo) + dot(k_lo, s_hi))
        mixed = jnp.concatenate([mixed[:, :N].reshape(W, 8, N), mixed[:, N:].reshape(W, 8, N)], axis=1)
        o_hi, o_lo = split(mixed)
        m_hi[:, here, :] = o_hi
        m_lo[:, here, :] = o_lo

    @pl.loop(0, W)
    def _(w):
        diag_r.at[w][...] = octets(jnp.where(places_i == places_j, r_buf.at[w][...], 0.0))

    permute_turn(0)

    @pl.when(seg >= 2)
    def _():
        chain_step()

    pre = prefix[...]
    pre_turned = left_cat(split(pre.T))
    load_b.wait()

    @pl.loop(0, W)
    def _(w):
        moved = exact(b_buf.at[w][...], prefix[...])
        diag_l.at[w][...] = octets(prefix[...] * moved)
        high, low = split(moved)
        c_hi.at[w][...] = high
        c_lo.at[w][...] = low

    side_r = exact(mix_full, diag_r[...].reshape(W8, N))
    diagonal[...] = exact(diag_l[...].reshape(W8, N), side_r, ((0,), (0,)))

    hop_left_cat = left_cat(split(hop_left[...]))
    group = 3 if W % 3 == 0 else 1

    def local_part(x_cat, first, last):
        @pl.loop(first, last)
        def _(g):
            base = g * group
            for i in range(group):
                w = base + i
                y = dot(left_cat((c_hi.at[w][...], c_lo.at[w][...])), x_cat)
                acc[...] += dot(left_cat(split(y)), right_cat((m_hi.at[w][...], m_lo.at[w][...])))

    steps = W // group
    norm = jnp.sqrt(reduce_end(0) + EPSILON)
    vec[...] = masked(psi[...]) / norm
    hop_scale = 1.0 / norm
    for t in range(DAV):
        x_cat = right_cat(split(vec[...]))
        acc[...] = jnp.zeros_like(acc)
        if t == 0:
            local_part(x_cat, 0, steps)
        else:
            local_part(x_cat, 0, steps // 2)
            permute_turn(t)
            local_part(x_cat, steps // 2, steps)
            norm = jnp.sqrt(reduce_end(2) + EPSILON)
            own_scale = own_norm / norm
            hop_scale = jnp.sqrt(reds[2][sources[0, sec]][0:1, 0:1] + EPSILON) / norm
        local = dot(pre_turned, right_cat(split(acc[...])))
        if t > 0:
            local = local * own_scale
            vec[...] = vec[...] * own_scale
        hop = dot(hop_left_cat, right_cat(split(permute_end(t))))
        image = masked(local + hop * hop_scale)
        vector = vec[...]
        reduce_start(2 * t + 1, total(vector * image))
        acc[...] = image
        rayleigh = reduce_end(2 * t + 1)
        vector = vec[...]
        residue = acc[...] - rayleigh * vector
        shifted = diagonal[...] - rayleigh
        update = vector - residue * shifted / (shifted * shifted + 1.0)
        squares = total(update * update)
        reduce_start(2 * t + 2, squares)
        if t < DAV - 1:
            own_norm = jnp.sqrt(squares + EPSILON)
            scaled = update / own_norm
            vec[...] = scaled
            permute_start(t + 1, dot(left_cat(split(scaled)), hop_right_cat))
        else:
            acc[...] = update
    norm = jnp.sqrt(reduce_end(2 * DAV) + EPSILON)
    out[...] = acc[...] * (math.sqrt(float(nsec * N * N)) / norm)

    for k in range(1, nseg):
        mix_copy(k, seg).wait_send()

    @pl.when(seg < nseg - 1)
    def _():
        for i in range(halves):
            chain_copy(i).wait_send()

    for k in range(1, nsec):
        for r in range(5):
            reduce_copy(r, k, sec).wait_send()
        for t in range(DAV):
            one_copy(t, k, other(sec, k, nsec), sec).wait_send()
            two_copy(t, k, other(sec, k, nsec), sec).wait_send()


def per_device(
    nseg, nsec,
    psi_init, boundary_env, right_env, transfer_blocks, transfer_mix, hop_left, hop_right, block_sizes, sources,
):
    W, N = right_env.shape[2], right_env.shape[3]
    rows = N // nsec
    WP = 128
    vmem = pl.BlockSpec(memory_space=pltpu.VMEM)
    smem = pl.BlockSpec(memory_space=pltpu.SMEM)
    hbm = pl.BlockSpec(memory_space=pl.ANY)
    square = pltpu.VMEM((N, N), F32)
    pieces = pltpu.VMEM((nsec, rows, N), F32)
    result = pl.pallas_call(
        functools.partial(kernel, nseg, nsec, W, N),
        out_shape=jax.ShapeDtypeStruct((N, N), F32),
        in_specs=[smem, smem, vmem, hbm, hbm, vmem, vmem, vmem, vmem],
        out_specs=vmem,
        scratch_shapes=[
            pltpu.VMEM((W, N, N), F32),
            pltpu.VMEM((W, N, N), F32),
            pltpu.VMEM((W, N, N), BF16),
            pltpu.VMEM((W, N, N), BF16),
            pltpu.VMEM((W, N, N), BF16),
            pltpu.VMEM((W, N, N), BF16),
            pltpu.VMEM((nseg, WP, WP), F32),
            square,
            square,
            pltpu.VMEM((W, 8, N), F32),
            pltpu.VMEM((W, 8, N), F32),
            square,
            square,
            square,
        ]
        + [pieces] * 8
        + [pltpu.VMEM((nsec, 8, 128), F32)] * 5
        + [
            pltpu.SemaphoreType.DMA((2,)),
            pltpu.SemaphoreType.DMA((nseg,)),
            pltpu.SemaphoreType.DMA((nseg,)),
            pltpu.SemaphoreType.DMA((2,)),
            pltpu.SemaphoreType.DMA((2,)),
            pltpu.SemaphoreType.DMA((2, nsec)),
            pltpu.SemaphoreType.DMA((2, nsec)),
            pltpu.SemaphoreType.DMA((2, nsec)),
            pltpu.SemaphoreType.DMA((2, nsec)),
            pltpu.SemaphoreType.DMA((5, nsec)),
            pltpu.SemaphoreType.DMA((5, nsec)),
        ],
        compiler_params=pltpu.CompilerParams(
            collective_id=0, has_side_effects=True, vmem_limit_bytes=48 * 1024 * 1024
        ),
    )(
        block_sizes[0], sources, psi_init[0, 0], boundary_env[0], right_env[0, 0], transfer_blocks[0, 0],
        transfer_mix[0], hop_left[0, 0], hop_right[0, 0],
    )
    return result[None, None]


def solution(mesh):
    return jax.shard_map(
        functools.partial(per_device, mesh.shape["seg"], mesh.shape["sec"]),
        mesh=mesh,
        in_specs=(
            P("seg", "sec", None, None),
            P("sec", None, None, None),
            P("seg", "sec", None, None, None),
            P("seg", "sec", None, None),
            P("seg", None, None),
            P("seg", "sec", None, None),
            P("seg", "sec", None, None),
            P("seg", None, None),
            P("seg", None),
        ),
        out_specs=P("seg", "sec", None, None),
        check_vma=False,
    )
```

```python
import functools
import math

import jax
import jax.numpy as jnp
from jax import lax
from jax.experimental import pallas as pl
from jax.experimental.pallas import tpu as pltpu
from jax.sharding import PartitionSpec as P

DAV = 2
EPSILON = 1e-06
HIGH = lax.Precision.HIGHEST
F32 = jnp.float32
BF16 = jnp.bfloat16
MESH = pl.DeviceIdType.MESH


def split(x):
    high = x.astype(BF16)
    return high, (x - high.astype(F32)).astype(BF16)


def left_cat(pair):
    high, low = pair
    return jnp.concatenate([high, high, low], axis=1)


def right_cat(pair):
    high, low = pair
    return jnp.concatenate([high, low, high], axis=0)


def dot(a, b):
    return jnp.dot(a, b, preferred_element_type=F32)


def exact(a, b, dims=((1,), (0,))):
    return lax.dot_general(a, b, (dims, ((), ())), precision=HIGH, preferred_element_type=F32)


def total(x):
    return jnp.sum(jnp.sum(x, axis=0, keepdims=True), axis=1, keepdims=True)


def octets(x):
    return jnp.sum(x.reshape(x.shape[0] // 8, 8, x.shape[1]), axis=0)


def kernel(
    nseg, nsec, W, N,
    sizes, sources, psi_in, boundary, right, own_in, mix_in, hop_left_in, hop_right_in,
    out,
    psi, own, mix, hop_left, hop_right,
    b_buf, r_buf, c_hi, c_lo, m_hi, m_lo, mixes, prefix, carry, diag_l, diag_r, diagonal, acc, vec,
    send_a, send_b, relay_a, relay_b, fwd_a, fwd_b, got_a, got_b,
    red0, red1, red2, red3, red4,
    load_sem, mix_send, mix_recv, chain_send, chain_recv,
    one_send, one_recv, two_send, two_recv, red_send, red_recv,
):
    seg, sec = lax.axis_index("seg"), lax.axis_index("sec")
    rows = N // nsec
    W8 = W * 8
    WP = mixes.shape[1]
    wide = -(-W // 8) * 8
    reds = (red0, red1, red2, red3, red4)
    sends, relays, fwds, gots = (send_a, send_b), (relay_a, relay_b), (fwd_a, fwd_b), (got_a, got_b)

    load_r = pltpu.make_async_copy(right, r_buf, load_sem.at[0])
    load_b = pltpu.make_async_copy(boundary, b_buf, load_sem.at[1])
    loads = [
        pltpu.make_async_copy(source, target, load_sem.at[2 + i])
        for i, (source, target) in enumerate(
            [(mix_in, mix), (own_in, own), (psi_in, psi), (hop_right_in, hop_right), (hop_left_in, hop_left)]
        )
    ]
    for load in loads:
        load.start()
    load_r.start()
    load_b.start()

    def other(index, step, count):
        return lax.rem(index + step, count)

    barrier = pltpu.get_barrier_semaphore()
    mixes[...] = jnp.zeros_like(mixes)
    for k in range(1, nsec):
        pl.semaphore_signal(barrier, inc=1, device_id={"sec": other(sec, k, nsec)}, device_id_type=MESH)
    for k in range(1, nseg):
        pl.semaphore_signal(barrier, inc=1, device_id={"seg": other(seg, k, nseg)}, device_id_type=MESH)

    loads[0].wait()
    mixes.at[seg][0:W, 0:W] = mix[...]
    loads[1].wait()

    @pl.when(seg == 0)
    def _():
        carry[...] = own[...]
        prefix[...] = jnp.where(
            lax.broadcasted_iota(jnp.int32, (N, N), 0) == lax.broadcasted_iota(jnp.int32, (N, N), 1), 1.0, 0.0
        )

    pl.semaphore_wait(barrier, nsec + nseg - 2)

    def mix_copy(k, slot):
        return pltpu.make_async_remote_copy(
            mixes.at[slot, pl.ds(0, wide)], mixes.at[slot, pl.ds(0, wide)],
            mix_send.at[k], mix_recv.at[k], device_id={"seg": other(seg, k, nseg)}, device_id_type=MESH,
        )

    for k in range(1, nseg):
        mix_copy(k, seg).start()

    halves = 2
    part = N // halves

    def chain_copy(i):
        return pltpu.make_async_remote_copy(
            carry.at[pl.ds(i * part, part)], prefix.at[pl.ds(i * part, part)],
            chain_send.at[i], chain_recv.at[i],
            device_id={"seg": lax.rem(seg + 1, nseg)}, device_id_type=MESH,
        )

    @pl.when(seg == 0)
    def _():
        for i in range(halves):
            chain_copy(i).start()

    def chain_step():
        for i in range(halves):
            chain_copy(i).wait_recv()

            @pl.when(seg < nseg - 1)
            def _():
                here = pl.ds(i * part, part)
                carry[here] = exact(prefix[here], own[...])
                chain_copy(i).start()

    def reduce_copy(r, k, slot):
        return pltpu.make_async_remote_copy(
            reds[r].at[slot], reds[r].at[slot], red_send.at[r, k], red_recv.at[r, k],
            device_id={"sec": other(sec, k, nsec)}, device_id_type=MESH,
        )

    def reduce_start(r, value):
        reds[r].at[sec][...] = jnp.broadcast_to(value, (8, 128))
        for k in range(1, nsec):
            reduce_copy(r, k, sec).start()

    def reduce_end(r):
        for k in range(1, nsec):
            reduce_copy(r, k, lax.rem(sec + nsec - k, nsec)).wait_recv()
        return jnp.sum(reds[r][...], axis=0)[0:1, 0:1]

    def one_copy(t, k, piece, slot):
        return pltpu.make_async_remote_copy(
            sends[t].at[piece], relays[t].at[slot], one_send.at[t, k], one_recv.at[t, k],
            device_id={"sec": other(sec, k, nsec)}, device_id_type=MESH,
        )

    def two_copy(t, k, piece, slot):
        return pltpu.make_async_remote_copy(
            fwds[t].at[piece], gots[t].at[slot], two_send.at[t, k], two_recv.at[t, k],
            device_id={"sec": other(sec, k, nsec)}, device_id_type=MESH,
        )

    def permute_start(t, value):
        sends[t][...] = value.reshape(nsec, rows, N)
        for k in range(1, nsec):
            one_copy(t, k, other(sec, k, nsec), sec).start()
        relays[t].at[sec][...] = sends[t].at[sec][...]

    def permute_turn(t):
        for k in range(1, nsec):
            one_copy(t, k, sec, lax.rem(sec + nsec - k, nsec)).wait_recv()
        for d in range(nsec):
            fwds[t][d] = relays[t][sources[0, d]]
        for k in range(1, nsec):
            two_copy(t, k, other(sec, k, nsec), sec).start()
        gots[t].at[sec][...] = fwds[t].at[sec][...]

    def permute_end(t):
        for k in range(1, nsec):
            two_copy(t, k, sec, lax.rem(sec + nsec - k, nsec)).wait_recv()
        return gots[t][...].reshape(N, N)

    places_i = lax.broadcasted_iota(jnp.int32, (N, N), 0)
    places_j = lax.broadcasted_iota(jnp.int32, (N, N), 1)

    def masked(x):
        return jnp.where((places_i < sizes[0, sec]) & (places_j < sizes[1, sec]), x, 0.0)

    loads[2].wait()
    loads[3].wait()
    hop_right_cat = right_cat(split(hop_right[...]))
    start = masked(psi[...])
    permute_start(0, dot(left_cat(split(start)), hop_right_cat))
    reduce_start(0, total(start * start))

    @pl.when((seg > 0) & (seg < 2))
    def _():
        chain_step()

    for k in range(1, nseg):
        mix_copy(k, lax.rem(seg + nseg - k, nseg)).wait_recv()
    prefix_mix = jnp.where(
        lax.broadcasted_iota(jnp.int32, (WP, WP), 0) == lax.broadcasted_iota(jnp.int32, (WP, WP), 1), 1.0, 0.0
    )
    for t in range(nseg - 1):
        prefix_mix = jnp.where(t < seg, exact(prefix_mix, mixes[t]), prefix_mix)
    spread = jnp.where(
        lax.broadcasted_iota(jnp.int32, (W8, WP), 0) // 8 == lax.broadcasted_iota(jnp.int32, (W8, WP), 1), 1.0, 0.0
    )
    mix_full = exact(exact(spread, prefix_mix), spread, ((1,), (1,)))
    same = (
        lax.broadcasted_iota(jnp.int32, (W8, W8), 0) % 8 == lax.broadcasted_iota(jnp.int32, (W8, W8), 1) % 8
    )
    k_hi, k_lo = split(jnp.where(same, mix_full, 0.0))
    load_r.wait()

    @pl.loop(0, N // 16)
    def _(c):
        here = pl.ds(pl.multiple_of(c * 16, 16), 16)
        chunk = r_buf[:, here, :]
        side = jnp.concatenate([chunk[:, 0:8].reshape(W8, N), chunk[:, 8:16].reshape(W8, N)], axis=1)
        s_hi, s_lo = split(side)
        mixed = dot(k_hi, s_hi) + (dot(k_hi, s_lo) + dot(k_lo, s_hi))
        mixed = jnp.concatenate([mixed[:, :N].reshape(W, 8, N), mixed[:, N:].reshape(W, 8, N)], axis=1)
        o_hi, o_lo = split(mixed)
        m_hi[:, here, :] = o_hi
        m_lo[:, here, :] = o_lo

    @pl.loop(0, W)
    def _(w):
        diag_r.at[w][...] = octets(jnp.where(places_i == places_j, r_buf.at[w][...], 0.0))

    permute_turn(0)

    @pl.when(seg >= 2)
    def _():
        chain_step()

    pre = prefix[...]
    p_hi, p_lo = split(pre)
    p_rest = (pre - p_hi.astype(F32) - p_lo.astype(F32)).astype(BF16)
    pre_cat = jnp.concatenate([p_hi, p_lo, p_rest, p_hi], axis=0)
    pre_turned = left_cat(split(pre.T))
    load_b.wait()

    @pl.loop(0, W)
    def _(w):
        e_hi, e_lo = split(b_buf.at[w][...])
        moved = dot(jnp.concatenate([e_hi, e_hi, e_hi, e_lo], axis=1), pre_cat)
        diag_l.at[w][...] = octets(prefix[...] * moved)
        high, low = split(moved)
        c_hi.at[w][...] = high
        c_lo.at[w][...] = low

    side_r = exact(mix_full, diag_r[...].reshape(W8, N))
    diagonal[...] = exact(diag_l[...].reshape(W8, N), side_r, ((0,), (0,)))

    loads[4].wait()
    hop_left_cat = left_cat(split(hop_left[...]))
    group = 3 if W % 3 == 0 else 1

    def local_part(x_cat, first, last):
        @pl.loop(first, last)
        def _(g):
            base = g * group
            for i in range(group):
                w = base + i
                y = dot(left_cat((c_hi.at[w][...], c_lo.at[w][...])), x_cat)
                acc[...] += dot(left_cat(split(y)), right_cat((m_hi.at[w][...], m_lo.at[w][...])))

    steps = W // group
    norm = jnp.sqrt(reduce_end(0) + EPSILON)
    vec[...] = masked(psi[...]) / norm
    hop_scale = 1.0 / norm
    for t in range(DAV):
        x_cat = right_cat(split(vec[...]))
        acc[...] = jnp.zeros_like(acc)
        if t == 0:
            local_part(x_cat, 0, steps)
        else:
            local_part(x_cat, 0, steps // 2)
            permute_turn(t)
            local_part(x_cat, steps // 2, steps)
            norm = jnp.sqrt(reduce_end(2) + EPSILON)
            own_scale = own_norm / norm
            hop_scale = jnp.sqrt(reds[2][sources[0, sec]][0:1, 0:1] + EPSILON) / norm
        local = dot(pre_turned, right_cat(split(acc[...])))
        if t > 0:
            local = local * own_scale
            vec[...] = vec[...] * own_scale
        hop = dot(hop_left_cat, right_cat(split(permute_end(t))))
        image = masked(local + hop * hop_scale)
        vector = vec[...]
        reduce_start(2 * t + 1, total(vector * image))
        acc[...] = image
        rayleigh = reduce_end(2 * t + 1)
        vector = vec[...]
        residue = acc[...] - rayleigh * vector
        shifted = diagonal[...] - rayleigh
        update = vector - residue * shifted / (shifted * shifted + 1.0)
        squares = total(update * update)
        reduce_start(2 * t + 2, squares)
        if t < DAV - 1:
            own_norm = jnp.sqrt(squares + EPSILON)
            scaled = update / own_norm
            vec[...] = scaled
            permute_start(t + 1, dot(left_cat(split(scaled)), hop_right_cat))
        else:
            acc[...] = update
    norm = jnp.sqrt(reduce_end(2 * DAV) + EPSILON)
    out[...] = acc[...] * (math.sqrt(float(nsec * N * N)) / norm)

    for k in range(1, nseg):
        mix_copy(k, seg).wait_send()

    @pl.when(seg < nseg - 1)
    def _():
        for i in range(halves):
            chain_copy(i).wait_send()

    for k in range(1, nsec):
        for r in range(5):
            reduce_copy(r, k, sec).wait_send()
        for t in range(DAV):
            one_copy(t, k, other(sec, k, nsec), sec).wait_send()
            two_copy(t, k, other(sec, k, nsec), sec).wait_send()


def per_device(
    nseg, nsec,
    psi_init, boundary_env, right_env, transfer_blocks, transfer_mix, hop_left, hop_right, block_sizes, sources,
):
    W, N = right_env.shape[2], right_env.shape[3]
    rows = N // nsec
    WP = 128
    vmem = pl.BlockSpec(memory_space=pltpu.VMEM)
    smem = pl.BlockSpec(memory_space=pltpu.SMEM)
    hbm = pl.BlockSpec(memory_space=pltpu.HBM)
    square = pltpu.VMEM((N, N), F32)
    pieces = pltpu.VMEM((nsec, rows, N), F32)
    result = pl.pallas_call(
        functools.partial(kernel, nseg, nsec, W, N),
        out_shape=jax.ShapeDtypeStruct((N, N), F32),
        in_specs=[smem, smem] + [hbm] * 7,
        out_specs=vmem,
        scratch_shapes=[
            square,
            square,
            pltpu.VMEM((W, W), F32),
            square,
            square,
            pltpu.VMEM((W, N, N), F32),
            pltpu.VMEM((W, N, N), F32),
            pltpu.VMEM((W, N, N), BF16),
            pltpu.VMEM((W, N, N), BF16),
            pltpu.VMEM((W, N, N), BF16),
            pltpu.VMEM((W, N, N), BF16),
            pltpu.VMEM((nseg, WP, WP), F32),
            square,
            square,
            pltpu.VMEM((W, 8, N), F32),
            pltpu.VMEM((W, 8, N), F32),
            square,
            square,
            square,
        ]
        + [pieces] * 8
        + [pltpu.VMEM((nsec, 8, 128), F32)] * 5
        + [
            pltpu.SemaphoreType.DMA((7,)),
            pltpu.SemaphoreType.DMA((nseg,)),
            pltpu.SemaphoreType.DMA((nseg,)),
            pltpu.SemaphoreType.DMA((2,)),
            pltpu.SemaphoreType.DMA((2,)),
            pltpu.SemaphoreType.DMA((2, nsec)),
            pltpu.SemaphoreType.DMA((2, nsec)),
            pltpu.SemaphoreType.DMA((2, nsec)),
            pltpu.SemaphoreType.DMA((2, nsec)),
            pltpu.SemaphoreType.DMA((5, nsec)),
            pltpu.SemaphoreType.DMA((5, nsec)),
        ],
        compiler_params=pltpu.CompilerParams(
            collective_id=0, has_side_effects=True, vmem_limit_bytes=(65536 - 320) * 1024
        ),
    )(
        block_sizes[0], sources, psi_init[0, 0], boundary_env[0], right_env[0, 0], transfer_blocks[0, 0],
        transfer_mix[0], hop_left[0, 0], hop_right[0, 0],
    )
    return result[None, None]


def solution(mesh):
    return jax.shard_map(
        functools.partial(per_device, mesh.shape["seg"], mesh.shape["sec"]),
        mesh=mesh,
        in_specs=(
            P("seg", "sec", None, None),
            P("sec", None, None, None),
            P("seg", "sec", None, None, None),
            P("seg", "sec", None, None),
            P("seg", None, None),
            P("seg", "sec", None, None),
            P("seg", "sec", None, None),
            P("seg", None, None),
            P("seg", None),
        ),
        out_specs=P("seg", "sec", None, None),
        check_vma=False,
    )
```

```python
import functools
import math

import jax
import jax.numpy as jnp
from jax import lax
from jax.experimental import pallas as pl
from jax.experimental.pallas import tpu as pltpu
from jax.sharding import PartitionSpec as P

DAV = 2
EPSILON = 1e-06
HIGH = lax.Precision.HIGHEST
F32 = jnp.float32
BF16 = jnp.bfloat16
MESH = pl.DeviceIdType.MESH


def split(x):
    high = x.astype(BF16)
    return high, (x - high.astype(F32)).astype(BF16)


def left_cat(pair):
    high, low = pair
    return jnp.concatenate([high, high, low], axis=1)


def right_cat(pair):
    high, low = pair
    return jnp.concatenate([high, low, high], axis=0)


def dot(a, b):
    return jnp.dot(a, b, preferred_element_type=F32)


def exact(a, b, dims=((1,), (0,))):
    return lax.dot_general(a, b, (dims, ((), ())), precision=HIGH, preferred_element_type=F32)


def total(x):
    return jnp.sum(jnp.sum(x, axis=0, keepdims=True), axis=1, keepdims=True)


def octets(x):
    return jnp.sum(x.reshape(x.shape[0] // 8, 8, x.shape[1]), axis=0)


def kernel(
    nseg, nsec, W, N,
    sizes, sources, psi_in, boundary, right, own_in, mix_in, hop_left_in, hop_right_in,
    out,
    psi, own, mix, hop_left, hop_right,
    b_buf, r_buf, c_hi, c_lo, m_hi, m_lo, mixes, prefix, carry, diag_l, diag_r, diagonal, acc, vec,
    send_a, send_b, relay_a, relay_b, fwd_a, fwd_b, got_a, got_b,
    red0, red1, red2, red3, red4,
    load_sem, mix_send, mix_recv, chain_send, chain_recv,
    one_send, one_recv, two_send, two_recv, red_send, red_recv,
):
    seg, sec = lax.axis_index("seg"), lax.axis_index("sec")
    rows = N // nsec
    W8 = W * 8
    WP = mixes.shape[1]
    wide = -(-W // 8) * 8
    reds = (red0, red1, red2, red3, red4)
    sends, relays, fwds, gots = (send_a, send_b), (relay_a, relay_b), (fwd_a, fwd_b), (got_a, got_b)

    load_r = pltpu.make_async_copy(right, r_buf, load_sem.at[0])
    load_b = pltpu.make_async_copy(boundary, b_buf, load_sem.at[1])
    loads = [
        pltpu.make_async_copy(source, target, load_sem.at[2 + i])
        for i, (source, target) in enumerate(
            [(mix_in, mix), (own_in, own), (psi_in, psi), (hop_right_in, hop_right), (hop_left_in, hop_left)]
        )
    ]
    for load in loads:
        load.start()
    load_r.start()
    load_b.start()

    def other(index, step, count):
        return lax.rem(index + step, count)

    barrier = pltpu.get_barrier_semaphore()
    mixes[...] = jnp.zeros_like(mixes)
    for k in range(1, nsec):
        pl.semaphore_signal(barrier, inc=1, device_id={"sec": other(sec, k, nsec)}, device_id_type=MESH)
    for k in range(1, nseg):
        pl.semaphore_signal(barrier, inc=1, device_id={"seg": other(seg, k, nseg)}, device_id_type=MESH)

    loads[0].wait()
    mixes.at[seg][0:W, 0:W] = mix[...]
    loads[1].wait()

    @pl.when(seg == 0)
    def _():
        carry[...] = own[...]
        prefix[...] = jnp.where(
            lax.broadcasted_iota(jnp.int32, (N, N), 0) == lax.broadcasted_iota(jnp.int32, (N, N), 1), 1.0, 0.0
        )

    places_i = lax.broadcasted_iota(jnp.int32, (N, N), 0)
    places_j = lax.broadcasted_iota(jnp.int32, (N, N), 1)

    def masked(x):
        return jnp.where((places_i < sizes[0, sec]) & (places_j < sizes[1, sec]), x, 0.0)

    loads[2].wait()
    loads[3].wait()
    hop_right_cat = right_cat(split(hop_right[...]))
    start = masked(psi[...])
    first_moving = dot(left_cat(split(start)), hop_right_cat)
    first_squares = total(start * start)
    pl.semaphore_wait(barrier, nsec + nseg - 2)

    def mix_copy(k, slot):
        return pltpu.make_async_remote_copy(
            mixes.at[slot, pl.ds(0, wide)], mixes.at[slot, pl.ds(0, wide)],
            mix_send.at[k], mix_recv.at[k], device_id={"seg": other(seg, k, nseg)}, device_id_type=MESH,
        )

    for k in range(1, nseg):
        mix_copy(k, seg).start()

    halves = 2
    part = N // halves

    def chain_copy(i):
        return pltpu.make_async_remote_copy(
            carry.at[pl.ds(i * part, part)], prefix.at[pl.ds(i * part, part)],
            chain_send.at[i], chain_recv.at[i],
            device_id={"seg": lax.rem(seg + 1, nseg)}, device_id_type=MESH,
        )

    @pl.when(seg == 0)
    def _():
        for i in range(halves):
            chain_copy(i).start()

    def chain_step():
        for i in range(halves):
            chain_copy(i).wait_recv()

            @pl.when(seg < nseg - 1)
            def _():
                here = pl.ds(i * part, part)
                carry[here] = exact(prefix[here], own[...])
                chain_copy(i).start()

    def reduce_copy(r, k, slot):
        return pltpu.make_async_remote_copy(
            reds[r].at[slot], reds[r].at[slot], red_send.at[r, k], red_recv.at[r, k],
            device_id={"sec": other(sec, k, nsec)}, device_id_type=MESH,
        )

    def reduce_start(r, value):
        reds[r].at[sec][...] = jnp.broadcast_to(value, (8, 128))
        for k in range(1, nsec):
            reduce_copy(r, k, sec).start()

    def reduce_end(r):
        for k in range(1, nsec):
            reduce_copy(r, k, lax.rem(sec + nsec - k, nsec)).wait_recv()
        return jnp.sum(reds[r][...], axis=0)[0:1, 0:1]

    def one_copy(t, k, piece, slot):
        return pltpu.make_async_remote_copy(
            sends[t].at[piece], relays[t].at[slot], one_send.at[t, k], one_recv.at[t, k],
            device_id={"sec": other(sec, k, nsec)}, device_id_type=MESH,
        )

    def two_copy(t, k, piece, slot):
        return pltpu.make_async_remote_copy(
            fwds[t].at[piece], gots[t].at[slot], two_send.at[t, k], two_recv.at[t, k],
            device_id={"sec": other(sec, k, nsec)}, device_id_type=MESH,
        )

    def permute_start(t, value):
        sends[t][...] = value.reshape(nsec, rows, N)
        for k in range(1, nsec):
            one_copy(t, k, other(sec, k, nsec), sec).start()
        relays[t].at[sec][...] = sends[t].at[sec][...]

    def permute_turn(t):
        for k in range(1, nsec):
            one_copy(t, k, sec, lax.rem(sec + nsec - k, nsec)).wait_recv()
        for d in range(nsec):
            fwds[t][d] = relays[t][sources[0, d]]
        for k in range(1, nsec):
            two_copy(t, k, other(sec, k, nsec), sec).start()
        gots[t].at[sec][...] = fwds[t].at[sec][...]

    def permute_end(t):
        for k in range(1, nsec):
            two_copy(t, k, sec, lax.rem(sec + nsec - k, nsec)).wait_recv()
        return gots[t][...].reshape(N, N)


    permute_start(0, first_moving)
    reduce_start(0, first_squares)

    @pl.when((seg > 0) & (seg < 2))
    def _():
        chain_step()

    for k in range(1, nseg):
        mix_copy(k, lax.rem(seg + nseg - k, nseg)).wait_recv()
    prefix_mix = jnp.where(
        lax.broadcasted_iota(jnp.int32, (WP, WP), 0) == lax.broadcasted_iota(jnp.int32, (WP, WP), 1), 1.0, 0.0
    )
    for t in range(nseg - 1):
        prefix_mix = jnp.where(t < seg, exact(prefix_mix, mixes[t]), prefix_mix)
    spread = jnp.where(
        lax.broadcasted_iota(jnp.int32, (W8, WP), 0) // 8 == lax.broadcasted_iota(jnp.int32, (W8, WP), 1), 1.0, 0.0
    )
    mix_full = exact(exact(spread, prefix_mix), spread, ((1,), (1,)))
    same = (
        lax.broadcasted_iota(jnp.int32, (W8, W8), 0) % 8 == lax.broadcasted_iota(jnp.int32, (W8, W8), 1) % 8
    )
    k_hi, k_lo = split(jnp.where(same, mix_full, 0.0))
    load_r.wait()

    @pl.loop(0, N // 16)
    def _(c):
        here = pl.ds(pl.multiple_of(c * 16, 16), 16)
        chunk = r_buf[:, here, :]
        side = jnp.concatenate([chunk[:, 0:8].reshape(W8, N), chunk[:, 8:16].reshape(W8, N)], axis=1)
        s_hi, s_lo = split(side)
        mixed = dot(k_hi, s_hi) + (dot(k_hi, s_lo) + dot(k_lo, s_hi))
        mixed = jnp.concatenate([mixed[:, :N].reshape(W, 8, N), mixed[:, N:].reshape(W, 8, N)], axis=1)
        o_hi, o_lo = split(mixed)
        m_hi[:, here, :] = o_hi
        m_lo[:, here, :] = o_lo

    @pl.loop(0, W)
    def _(w):
        diag_r.at[w][...] = octets(jnp.where(places_i == places_j, r_buf.at[w][...], 0.0))

    @pl.when(seg >= 2)
    def _():
        chain_step()

    pre = prefix[...]
    p_hi, p_lo = split(pre)
    p_rest = (pre - p_hi.astype(F32) - p_lo.astype(F32)).astype(BF16)
    pre_cat = jnp.concatenate([p_hi, p_lo, p_rest, p_hi], axis=0)
    pre_turned = left_cat(split(pre.T))
    load_b.wait()

    def left_part(first, last):
        @pl.loop(first, last)
        def _(w):
            e_hi, e_lo = split(b_buf.at[w][...])
            moved = dot(jnp.concatenate([e_hi, e_hi, e_hi, e_lo], axis=1), pre_cat)
            diag_l.at[w][...] = octets(prefix[...] * moved)
            high, low = split(moved)
            c_hi.at[w][...] = high
            c_lo.at[w][...] = low

    left_part(0, W // 2)
    permute_turn(0)
    left_part(W // 2, W)

    side_r = exact(mix_full, diag_r[...].reshape(W8, N))
    diagonal[...] = exact(diag_l[...].reshape(W8, N), side_r, ((0,), (0,)))

    loads[4].wait()
    hop_left_cat = left_cat(split(hop_left[...]))
    group = 3 if W % 3 == 0 else 1

    def local_part(x_cat, first, last):
        @pl.loop(first, last)
        def _(g):
            base = g * group
            for i in range(group):
                w = base + i
                y = dot(left_cat((c_hi.at[w][...], c_lo.at[w][...])), x_cat)
                acc[...] += dot(left_cat(split(y)), right_cat((m_hi.at[w][...], m_lo.at[w][...])))

    steps = W // group
    norm = jnp.sqrt(reduce_end(0) + EPSILON)
    vec[...] = masked(psi[...]) / norm
    hop_scale = 1.0 / norm
    for t in range(DAV):
        x_cat = right_cat(split(vec[...]))
        acc[...] = jnp.zeros_like(acc)
        if t == 0:
            local_part(x_cat, 0, steps)
        else:
            local_part(x_cat, 0, steps // 2)
            permute_turn(t)
            local_part(x_cat, steps // 2, steps)
            norm = jnp.sqrt(reduce_end(2) + EPSILON)
            own_scale = own_norm / norm
            hop_scale = jnp.sqrt(reds[2][sources[0, sec]][0:1, 0:1] + EPSILON) / norm
        local = dot(pre_turned, right_cat(split(acc[...])))
        if t > 0:
            local = local * own_scale
            vec[...] = vec[...] * own_scale
        hop = dot(hop_left_cat, right_cat(split(permute_end(t))))
        image = masked(local + hop * hop_scale)
        vector = vec[...]
        reduce_start(2 * t + 1, total(vector * image))
        acc[...] = image
        rayleigh = reduce_end(2 * t + 1)
        vector = vec[...]
        residue = acc[...] - rayleigh * vector
        shifted = diagonal[...] - rayleigh
        update = vector - residue * shifted / (shifted * shifted + 1.0)
        squares = total(update * update)
        reduce_start(2 * t + 2, squares)
        if t < DAV - 1:
            own_norm = jnp.sqrt(squares + EPSILON)
            scaled = update / own_norm
            vec[...] = scaled
            permute_start(t + 1, dot(left_cat(split(scaled)), hop_right_cat))
        else:
            acc[...] = update
    norm = jnp.sqrt(reduce_end(2 * DAV) + EPSILON)
    out[...] = acc[...] * (math.sqrt(float(nsec * N * N)) / norm)

    for k in range(1, nseg):
        mix_copy(k, seg).wait_send()

    @pl.when(seg < nseg - 1)
    def _():
        for i in range(halves):
            chain_copy(i).wait_send()

    for k in range(1, nsec):
        for r in range(5):
            reduce_copy(r, k, sec).wait_send()
        for t in range(DAV):
            one_copy(t, k, other(sec, k, nsec), sec).wait_send()
            two_copy(t, k, other(sec, k, nsec), sec).wait_send()


def per_device(
    nseg, nsec,
    psi_init, boundary_env, right_env, transfer_blocks, transfer_mix, hop_left, hop_right, block_sizes, sources,
):
    W, N = right_env.shape[2], right_env.shape[3]
    rows = N // nsec
    WP = 128
    vmem = pl.BlockSpec(memory_space=pltpu.VMEM)
    smem = pl.BlockSpec(memory_space=pltpu.SMEM)
    hbm = pl.BlockSpec(memory_space=pltpu.HBM)
    square = pltpu.VMEM((N, N), F32)
    pieces = pltpu.VMEM((nsec, rows, N), F32)
    result = pl.pallas_call(
        functools.partial(kernel, nseg, nsec, W, N),
        out_shape=jax.ShapeDtypeStruct((N, N), F32),
        in_specs=[smem, smem] + [hbm] * 7,
        out_specs=vmem,
        scratch_shapes=[
            square,
            square,
            pltpu.VMEM((W, W), F32),
            square,
            square,
            pltpu.VMEM((W, N, N), F32),
            pltpu.VMEM((W, N, N), F32),
            pltpu.VMEM((W, N, N), BF16),
            pltpu.VMEM((W, N, N), BF16),
            pltpu.VMEM((W, N, N), BF16),
            pltpu.VMEM((W, N, N), BF16),
            pltpu.VMEM((nseg, WP, WP), F32),
            square,
            square,
            pltpu.VMEM((W, 8, N), F32),
            pltpu.VMEM((W, 8, N), F32),
            square,
            square,
            square,
        ]
        + [pieces] * 8
        + [pltpu.VMEM((nsec, 8, 128), F32)] * 5
        + [
            pltpu.SemaphoreType.DMA((7,)),
            pltpu.SemaphoreType.DMA((nseg,)),
            pltpu.SemaphoreType.DMA((nseg,)),
            pltpu.SemaphoreType.DMA((2,)),
            pltpu.SemaphoreType.DMA((2,)),
            pltpu.SemaphoreType.DMA((2, nsec)),
            pltpu.SemaphoreType.DMA((2, nsec)),
            pltpu.SemaphoreType.DMA((2, nsec)),
            pltpu.SemaphoreType.DMA((2, nsec)),
            pltpu.SemaphoreType.DMA((5, nsec)),
            pltpu.SemaphoreType.DMA((5, nsec)),
        ],
        compiler_params=pltpu.CompilerParams(
            collective_id=0, has_side_effects=True, vmem_limit_bytes=(65536 - 320) * 1024
        ),
    )(
        block_sizes[0], sources, psi_init[0, 0], boundary_env[0], right_env[0, 0], transfer_blocks[0, 0],
        transfer_mix[0], hop_left[0, 0], hop_right[0, 0],
    )
    return result[None, None]


def solution(mesh):
    return jax.shard_map(
        functools.partial(per_device, mesh.shape["seg"], mesh.shape["sec"]),
        mesh=mesh,
        in_specs=(
            P("seg", "sec", None, None),
            P("sec", None, None, None),
            P("seg", "sec", None, None, None),
            P("seg", "sec", None, None),
            P("seg", None, None),
            P("seg", "sec", None, None),
            P("seg", "sec", None, None),
            P("seg", None, None),
            P("seg", None),
        ),
        out_specs=P("seg", "sec", None, None),
        check_vma=False,
    )
```
